512 devices in a mesh: row: 32 (over z, y_hi), col: 16 (over x, y_lo, core).
Axes of the slice: x: 4, y: 8 (y_hi: 4, y_lo: 2; y = y_hi * 2 + y_lo), z: 8, core: 2. Of those that a mesh axis runs over, the one named last changes fastest.
Arguments:
- momentum: bfloat16 [4096, 14336], P('row', 'col'), may hold values from -0.098552583 to 0.098552583
Outputs:
- update: float32 [4096, 14336], P('row', 'col')
The draws below stay inside these ranges and needn't reach their ends.
All inputs are finite; a program needn't handle non-finite values.
Results may differ from the reference program's by a relative error of at most 0.0048.
Values may be sent and summed in bfloat16 or wider, within the bound.
A program may use at most 64 MiB of HBM per device.

```python
import math
import jax
import jax.numpy as jnp

M = 4096
N = 14336


def draw_momentum(key, part):
    key = jax.random.fold_in(key, 11)
    first, second, third = jax.random.split(key, 3)
    base = jnp.clip(jax.random.normal(third, (M, N), jnp.float32), -5.0, 5.0)
    lowest, highest = (math.log(0.5), math.log(2.0))
    row_scale = jnp.exp(jax.random.uniform(first, (M, 1), jnp.float32, lowest, highest))
    col_scale = jnp.exp(jax.random.uniform(second, (1, N), jnp.float32, 0.0, math.log(10.0)))
    return (0.118 / math.sqrt(N) * base * row_scale * col_scale).astype(jnp.bfloat16)


def setup_inputs(seed: int = 0) -> dict:
    streams_of = jax.random.split(jax.random.key(seed), 2)
    momentum = draw_momentum(jax.random.fold_in(streams_of[1], 71), 0)
    return {"momentum": momentum}


quintic_a = 3.4445
quintic_b = -4.775
quintic_c = 2.0315

def reference(momentum):
    gram = jnp.dot(momentum, momentum.T, preferred_element_type=jnp.float32)
    gram_half = gram.astype(jnp.bfloat16)
    square = jnp.dot(gram_half, gram_half, preferred_element_type=jnp.float32)
    poly = (quintic_b * gram_half.astype(jnp.float32) + quintic_c * square).astype(jnp.bfloat16)
    product = jnp.dot(poly, momentum, preferred_element_type=jnp.float32)
    return math.sqrt(max(M, N)) * (quintic_a * momentum.astype(jnp.float32) + product)
```

```python
import math

import jax
import jax.numpy as jnp
from jax import lax
from jax.experimental import pallas as pl
from jax.experimental.pallas import tpu as pltpu
from jax.sharding import PartitionSpec as P

M = 4096
N = 14336
quintic_a = 3.4445
quintic_b = -4.775
quintic_c = 2.0315

NZ, NYH, NX, NYL = 8, 4, 4, 2
NY = NYH * NYL
R = 128
C = 896
H = R // 2
W = 256
CZ = 384
CY = C - CZ
SEMS = 200

F32 = jnp.float32
BF16 = jnp.bfloat16


def kernel(
    x_ref, out_ref,
    xi, xj, acc, sib_out, sib_in, rs_out, rs_in, ga, gb, pb, pt,
    zs_out, zs_in, ys_out, ys_in, zown, yown,
    send_sems, recv_sems,
):
    row = lax.axis_index("row")
    col = lax.axis_index("col")
    z, yh = row // NYH, row % NYH
    q, h = col // 2, col % 2
    x, yl = q // NYL, q % NYL
    y = yh * NYL + yl

    def device(z=z, y=y, x=x, h=h):
        return (z * NYH + y // NYL, (x * NYL + y % NYL) * 2 + h)

    def zmod(d):
        return (z + d + NZ) % NZ

    def ymod(d):
        return (y + d + NY) % NY

    def yhmod(d):
        return (yh + d + NYH) % NYH

    z_dev = {1: device(z=zmod(1)), -1: device(z=zmod(-1))}
    y_dev = {1: device(y=ymod(1)), -1: device(y=ymod(-1))}
    yh_dev = {1: device(y=ymod(2)), -1: device(y=ymod(-2))}
    sibling = device(h=1 - h)

    def q_dev(k):
        dx, dy = k // 2, k % 2
        return device(x=(x + dx) % NX, y=yh * NYL + (yl + dy) % NYL)

    def q_of(k):
        dx, dy = k // 2, k % 2
        return ((x + dx) % NX) * NYL + (yl + dy) % NYL

    pending = []
    count = [0]

    def send(src, dst, to):
        n = count[0]
        count[0] += 1
        copy = pltpu.make_async_remote_copy(
            src_ref=src, dst_ref=dst, send_sem=send_sems.at[n], recv_sem=recv_sems.at[n],
            device_id=to, device_id_type=pl.DeviceIdType.MESH,
        )
        copy.start()
        pending.append(copy)
        return copy

    barrier = pltpu.get_barrier_semaphore()
    partners = [z_dev[1], z_dev[-1], yh_dev[1], yh_dev[-1], y_dev[1], y_dev[-1], sibling]
    partners += [q_dev(k) for k in range(1, 8)]
    for partner in partners:
        pl.semaphore_signal(barrier, inc=1, device_id=partner, device_id_type=pl.DeviceIdType.MESH)
    pl.semaphore_wait(barrier, len(partners))

    top, low = pl.ds(0, H), pl.ds(H, H)
    halves = (top, low)
    zc, yc = {}, {}
    for c in range(2):
        for d in (1, -1):
            zc[d, 1, c] = send(x_ref.at[halves[c]], xi.at[z, halves[c]], z_dev[d])
            yc[d, 1, c] = send(x_ref.at[halves[c]], xj.at[yh, halves[c]], yh_dev[d])
    xi[z] = x_ref[...]
    xj[yh] = x_ref[...]

    def z_step(s, c):
        for d in (1, -1):
            if (d, s, c) not in zc:
                continue
            zc[d, s, c].wait_recv()
            if s < 3 or (s == 3 and c == (0 if d == 1 else 1)):
                held = xi.at[zmod(-d * s), halves[c]]
                zc[d, s + 1, c] = send(held, held, z_dev[d])

    def y_step(s, c):
        for d in (1, -1):
            if (d, s, c) not in yc:
                continue
            yc[d, s, c].wait_recv()
            if s == 1 and c == (0 if d == 1 else 1):
                held = xj.at[yhmod(-d), halves[c]]
                yc[d, 2, c] = send(held, held, yh_dev[d])

    z_step(1, 0)
    z_step(1, 1)
    y_step(1, 0)
    z_step(2, 0)
    z_step(2, 1)
    y_step(1, 1)
    z_step(3, 0)
    z_step(3, 1)
    y_step(2, 0)
    y_step(2, 1)

    def gram(zz, own):
        left = xi[zz]
        for half in range(2):
            right = xj[2 * half : 2 * half + 2].reshape(W, C)
            value = lax.dot_general(left, right, (((1,), (1,)), ((), ())), preferred_element_type=F32)

            @pl.when(h == half)
            def _():
                acc[zz] = value

            @pl.when(h != half)
            def _():
                sib_out[zz] = value

    z_step(4, 0)
    z_step(4, 1)
    sib = {}
    order = [1, 2, 3, 4, 5, 6, 7, 0]
    for k in order:
        zz = q_of(k)
        gram(zz, None)
        sib[k] = send(sib_out.at[zz], sib_in.at[zz], sibling)
    rs = {}
    for k in order:
        zz = q_of(k)
        sib[k].wait_recv()
        total = acc[zz] + sib_in[zz]
        if k:
            rs_out[k] = total.astype(BF16)
            rs[k] = send(rs_out.at[k], rs_in.at[k], q_dev(k))
        else:
            acc[q] = total
    total = acc[q]
    for k in range(1, 8):
        rs[k].wait_recv()
        total = total + rs_in[k].astype(F32)
    gram_own = total.astype(BF16)
    gb[x, y] = gram_own
    ga[z, h] = gram_own

    bc, ac, bx, ax, gz, gs = {}, {}, {}, {}, {}, {}
    quarters = (pl.ds(H, H // 2), pl.ds(H + H // 2, H // 2))
    for d in (1, -1):
        bc[d, 1] = send(gb.at[x, y, low], gb.at[x, y, low], y_dev[d])
    for dx in (1, 3, 2):
        ax[dx] = send(gb.at[x, y, top], gb.at[x, y, top], device(x=(x + dx) % NX))
    for d in (1, -1):
        ac[d, 1, 0] = send(gb.at[x, y, top], gb.at[x, y, top], y_dev[d])
    for d in (1, -1):
        gz[d, 1] = send(ga.at[z, h], ga.at[z, h], z_dev[d])
    for dx in (1, 3, 2):
        bx[0, dx] = send(gb.at[x, y, low], gb.at[x, y, low], device(x=(x + dx) % NX))
    gs[0] = send(ga.at[z, h], ga.at[z, h], sibling)
    zrows = (pl.ds(0, H), pl.ds(H, H))

    def b_step(s):
        for d in (1, -1):
            bc[d, s].wait_recv()
            if s < 3:
                held = gb.at[x, ymod(-d * s), low]
                bc[d, s + 1] = send(held, held, y_dev[d])
            elif s == 3:
                held = gb.at[x, ymod(-d * s), quarters[0 if d == 1 else 1]]
                bc[d, 4] = send(held, held, y_dev[d])
        for d in (1, -1) if s < 4 else (1,):
            held = gb.at[x, ymod(-d * s), low]
            for dx in (1, 3, 2):
                bx[d * s, dx] = send(held, held, device(x=(x + dx) % NX))

    def gz_step(s):
        for d in (1, -1):
            gz[d, s].wait_recv()
            if s < 3:
                held = ga.at[zmod(-d * s), h]
                gz[d, s + 1] = send(held, held, z_dev[d])
            elif s == 3:
                held = ga.at[zmod(-d * s), h, zrows[0 if d == 1 else 1]]
                gz[d, 4] = send(held, held, z_dev[d])
        for d in (1, -1) if s < 4 else (1,):
            held = ga.at[zmod(-d * s), h]
            gs[d * s] = send(held, held, sibling)

    def a_step(s, rx):
        for d in (1, -1):
            if s == 0:
                if d == 1:
                    ax[rx].wait_recv()
            elif (d, s, rx) in ac:
                ac[d, s, rx].wait_recv()
            else:
                continue
            if s < 3 or (s == 3 and (rx in (0, 1)) == (d == 1)):
                held = gb.at[(x - rx + NX) % NX, ymod(-d * s), top]
                ac[d, s + 1, rx] = send(held, held, y_dev[d])

    b_step(1)
    for rx in (1, 3, 2):
        a_step(0, rx)
    gz_step(1)
    a_step(1, 0)
    b_step(2)
    for rx in (1, 3, 2):
        a_step(1, rx)
    gz_step(2)
    a_step(2, 0)
    b_step(3)
    for rx in (1, 3, 2):
        a_step(2, rx)
    gz_step(3)
    b_step(4)
    gz_step(4)
    for rx in (0, 1, 3, 2):
        a_step(3, rx)
    for rx in (0, 1, 3, 2):
        a_step(4, rx)
    for copy in bx.values():
        copy.wait_recv()
    for copy in gs.values():
        copy.wait_recv()

    def square(qq, total):
        xx, yy = qq // NYL, qq % NYL
        for half in range(2):
            right = jnp.concatenate(
                [gb[xx, 4 * half + yy], gb[xx, 4 * half + 2 + yy]], axis=0
            )
            total = total + jnp.dot(ga[qq, half], right, preferred_element_type=F32)
        return total

    total = jnp.zeros((R, W), F32)
    for qq in range(8):
        total = square(qq, total)
    poly = (quintic_b * gb[x, y].astype(F32) + quintic_c * total).astype(BF16)
    pb[q, h] = poly

    pc, ps = {}, {}
    for k in (2, 6, 1, 4, 3, 7, 5):
        pc[k] = send(pb.at[q, h], pb.at[q, h], q_dev(k))
    ps[0] = send(pb.at[q, h], pb.at[q, h], sibling)
    for k in (2, 6, 1, 4, 3, 7, 5):
        dx, dy = k // 2, k % 2
        held = pb.at[((x - dx + NX) % NX) * NYL + (yl + dy) % NYL, h]
        pc[k].wait_recv()
        ps[k] = send(held, held, sibling)
    for copy in ps.values():
        copy.wait_recv()

    for qq in range(8):
        for half in range(2):
            turned = pb[qq, half].astype(F32).T.astype(BF16)
            for part in range(2):
                pt[2 * half + part, :, qq * R : (qq + 1) * R] = turned[part * R : (part + 1) * R]

    def z_part(zz, rows):
        value = 0.0
        for half in range(2):
            right = xj[2 * half : 2 * half + 2, :, 0:CZ].reshape(W, CZ)
            value = value + jnp.dot(pb[zz, half, rows], right, preferred_element_type=F32)
        return value

    def y_part(yy, rows):
        right = xi[:, :, CZ:C].reshape(NZ * R, CY)
        return jnp.dot(pt[yy, rows], right, preferred_element_type=F32)

    zr, yr = {}, {}

    def first(d):
        return 0 if d == 1 else 1

    def z_send(d, s, c, value):
        n = 0 if d == 1 else 1
        zs_out[n, s, halves[c]] = value.astype(BF16)
        zr[d, s, c] = send(zs_out.at[n, s, halves[c]], zs_in.at[n, s, halves[c]], z_dev[d])

    def y_send(d, s, c, value):
        n = 0 if d == 1 else 1
        ys_out[n, s, halves[c]] = value.astype(BF16)
        yr[d, s, c] = send(ys_out.at[n, s, halves[c]], ys_in.at[n, s, halves[c]], yh_dev[d])

    def z_got(d, s, c):
        zr[d, s, c].wait_recv()
        return zs_in[0 if d == 1 else 1, s, halves[c]].astype(F32)

    def y_got(d, s, c):
        yr[d, s, c].wait_recv()
        return ys_in[0 if d == 1 else 1, s, halves[c]].astype(F32)

    for d in (1, -1):
        z_send(d, 0, first(d), z_part(zmod(4 * d), halves[first(d)]))
    for d in (1, -1):
        y_send(d, 0, first(d), y_part(yhmod(2 * d), halves[first(d)]))
    for d in (1, -1):
        z_send(d, 1, 1 - first(d), z_part(zmod(3 * d), halves[1 - first(d)]))
    for d in (1, -1):
        y_send(d, 1, 1 - first(d), y_part(yhmod(d), halves[1 - first(d)]))
    for d in (1, -1):
        c = first(d)
        z_send(d, 1, c, z_part(zmod(3 * d), halves[c]) + z_got(d, 0, c))
    for d in (1, -1):
        c = 1 - first(d)
        z_send(d, 2, c, z_part(zmod(2 * d), halves[c]) + z_got(d, 1, c))
    for d in (1, -1):
        c = first(d)
        y_send(d, 1, c, y_part(yhmod(d), halves[c]) + y_got(d, 0, c))
    for d in (1, -1):
        c = first(d)
        z_send(d, 2, c, z_part(zmod(2 * d), halves[c]) + z_got(d, 1, c))
    for d in (1, -1):
        c = 1 - first(d)
        z_send(d, 3, c, z_part(zmod(d), halves[c]) + z_got(d, 2, c))
    for d in (1, -1):
        c = first(d)
        z_send(d, 3, c, z_part(zmod(d), halves[c]) + z_got(d, 2, c))

    zown[...] = z_part(z, pl.ds(0, R))
    yown[...] = y_part(yh, pl.ds(0, R))
    scale = math.sqrt(max(M, N))
    for c in (0, 1):
        rows = halves[c]
        value = yown[rows] + y_got(1, 1, c) + y_got(-1, 1, c)
        out_ref[rows, CZ:C] = scale * (quintic_a * x_ref[rows, CZ:C].astype(F32) + value)
    for c in (0, 1):
        rows = halves[c]
        value = zown[rows] + z_got(1, 3, c) + z_got(-1, 3, c)
        out_ref[rows, 0:CZ] = scale * (quintic_a * x_ref[rows, 0:CZ].astype(F32) + value)

    for copy in pending:
        copy.wait_send()


def per_device(momentum):
    return pl.pallas_call(
        kernel,
        out_shape=jax.ShapeDtypeStruct((R, C), F32),
        in_specs=[pl.BlockSpec(memory_space=pltpu.VMEM)],
        out_specs=pl.BlockSpec(memory_space=pltpu.VMEM),
        scratch_shapes=[
            pltpu.VMEM((NZ, R, C), BF16),
            pltpu.VMEM((NYH, R, C), BF16),
            pltpu.VMEM((NZ, R, W), F32),
            pltpu.VMEM((NZ, R, W), F32),
            pltpu.VMEM((NZ, R, W), F32),
            pltpu.VMEM((NZ, R, W), BF16),
            pltpu.VMEM((NZ, R, W), BF16),
            pltpu.VMEM((NZ, 2, R, W), BF16),
            pltpu.VMEM((NX, NY, R, W), BF16),
            pltpu.VMEM((NZ, 2, R, W), BF16),
            pltpu.VMEM((NYH, R, NZ * R), BF16),
            pltpu.VMEM((2, 4, R, CZ), BF16),
            pltpu.VMEM((2, 4, R, CZ), BF16),
            pltpu.VMEM((2, 2, R, CY), BF16),
            pltpu.VMEM((2, 2, R, CY), BF16),
            pltpu.VMEM((R, CZ), F32),
            pltpu.VMEM((R, CY), F32),
            pltpu.SemaphoreType.DMA((SEMS,)),
            pltpu.SemaphoreType.DMA((SEMS,)),
        ],
        compiler_params=pltpu.CompilerParams(
            collective_id=0, has_side_effects=True, vmem_limit_bytes=48 * 1024 * 1024
        ),
        cost_estimate=pl.CostEstimate(flops=2200000000, bytes_accessed=1000000, transcendentals=0),
        name="newton_schulz",
    )(momentum)


def solution(mesh):
    return jax.shard_map(
        per_device, mesh=mesh, in_specs=(P("row", "col"),), out_specs=P("row", "col"), check_vma=False
    )
```

```python
import math

import jax
import jax.numpy as jnp
from jax import lax
from jax.experimental import pallas as pl
from jax.experimental.pallas import tpu as pltpu
from jax.sharding import PartitionSpec as P

M = 4096
N = 14336
quintic_a = 3.4445
quintic_b = -4.775
quintic_c = 2.0315

NZ, NYH, NX, NYL = 8, 4, 4, 2
NY = NYH * NYL
R = 128
C = 896
H = R // 2
W = 256
CZ = 384
CY = C - CZ
SEMS = 230
CHZ = 4
CHY = 2
HA = 48

F32 = jnp.float32
BF16 = jnp.bfloat16


def kernel(
    x_ref, out_ref,
    xi, xj, acc, sib_out, sib_in, rs_own, rs_out, rs_in, ga, gb, pb, pt,
    zs_out, zs_in, ys_out, ys_in, zp, yp,
    send_sems, recv_sems, rs_send, rs_recv, sib_send, sib_recv, local_sems,
):
    row = lax.axis_index("row")
    col = lax.axis_index("col")
    z, yh = row // NYH, row % NYH
    q, h = col // 2, col % 2
    x, yl = q // NYL, q % NYL
    y = yh * NYL + yl

    def device(z=z, y=y, x=x, h=h):
        return (z * NYH + y // NYL, (x * NYL + y % NYL) * 2 + h)

    def zmod(d):
        return (z + d + NZ) % NZ

    def ymod(d):
        return (y + d + NY) % NY

    def yhmod(d):
        return (yh + d + NYH) % NYH

    z_dev = {1: device(z=zmod(1)), -1: device(z=zmod(-1))}
    y_dev = {1: device(y=ymod(1)), -1: device(y=ymod(-1))}
    yh_dev = {1: device(y=ymod(2)), -1: device(y=ymod(-2))}
    sibling = device(h=1 - h)

    def q_dev(k):
        dx, dy = k // 2, k % 2
        return device(x=(x + dx) % NX, y=yh * NYL + (yl + dy) % NYL)

    def q_of(k):
        dx, dy = k // 2, k % 2
        return ((x + dx) % NX) * NYL + (yl + dy) % NYL

    pending = []
    count = [0]

    def send(src, dst, to):
        n = count[0]
        count[0] += 1
        copy = pltpu.make_async_remote_copy(
            src_ref=src, dst_ref=dst, send_sem=send_sems.at[n], recv_sem=recv_sems.at[n],
            device_id=to, device_id_type=pl.DeviceIdType.MESH,
        )
        copy.start()
        pending.append(copy)
        return copy

    barrier = pltpu.get_barrier_semaphore()
    partners = [z_dev[1], z_dev[-1], yh_dev[1], yh_dev[-1], y_dev[1], y_dev[-1], sibling]
    partners += [q_dev(k) for k in range(1, 8)] + [device(z=zmod(2)), device(z=zmod(-2))]
    for partner in partners:
        pl.semaphore_signal(barrier, inc=1, device_id=partner, device_id_type=pl.DeviceIdType.MESH)
    pl.semaphore_wait(barrier, len(partners))

    top, low = pl.ds(0, H), pl.ds(H, H)
    halves = (top, low)
    cz = [pl.ds(c * R // CHZ, R // CHZ) for c in range(CHZ)]
    cy = [pl.ds(c * R // CHY, R // CHY) for c in range(CHY)]
    zc, yc = {}, {}
    for c in range(max(CHZ, CHY)):
        for d in (1, -1):
            if c < CHZ:
                zc[d, 1, c] = send(x_ref.at[cz[c]], xi.at[z, cz[c]], z_dev[d])
        for d in (1, -1):
            if c < CHY:
                yc[d, 1, c] = send(x_ref.at[cy[c]], xj.at[yh, cy[c]], yh_dev[d])
    local = [
        pltpu.make_async_copy(x_ref, xi.at[z], local_sems.at[0]),
        pltpu.make_async_copy(x_ref, xj.at[yh], local_sems.at[1]),
    ]
    for copy in local:
        copy.start()

    def z_step(s, c):
        for d in (1, -1):
            if (d, s, c) not in zc:
                continue
            zc[d, s, c].wait_recv()
            if s < 3 or (s == 3 and (2 * c < CHZ) == (d == 1)):
                held = xi.at[zmod(-d * s), cz[c]]
                zc[d, s + 1, c] = send(held, held, z_dev[d])

    def y_step(s, c):
        for d in (1, -1):
            if (d, s, c) not in yc:
                continue
            yc[d, s, c].wait_recv()
            if s == 1 and (2 * c < CHY) == (d == 1):
                held = xj.at[yhmod(-d), cy[c]]
                yc[d, 2, c] = send(held, held, yh_dev[d])

    def sib_copy(zz, yb):
        return pltpu.make_async_remote_copy(
            src_ref=sib_out.at[zz, yb], dst_ref=sib_in.at[zz, yb],
            send_sem=sib_send.at[zz, yb], recv_sem=sib_recv.at[zz, yb],
            device_id=sibling, device_id_type=pl.DeviceIdType.MESH,
        )

    def rs_copy(to, slot, bit):
        return pltpu.make_async_remote_copy(
            src_ref=rs_out.at[to, bit], dst_ref=rs_in.at[slot, bit],
            send_sem=rs_send.at[to, bit], recv_sem=rs_recv.at[slot, bit],
            device_id=device(x=to // NYL, y=yh * NYL + to % NYL),
            device_id_type=pl.DeviceIdType.MESH,
        )

    def gram(offsets, blocks):
        left = jnp.concatenate([xi[zmod(a)] for a in offsets], axis=0)
        right = jnp.concatenate([xj[yhmod(b)] for b in blocks], axis=0)
        value = lax.dot_general(left, right, (((1,), (1,)), ((), ())), preferred_element_type=F32)
        for n, a in enumerate(offsets):
            for m, b in enumerate(blocks):
                part = value[n * R : (n + 1) * R, m * R : (m + 1) * R]
                zz, yb = zmod(a), yhmod(b)

                @pl.when(yb // 2 == h)
                def _():
                    acc[zz, yb % 2] = part

                @pl.when(yb // 2 != h)
                def _():
                    sib_out[zz, yb] = part
                    sib_copy(zz, yb).start()

    def rs_step(offsets, blocks):
        for a in offsets:
            for b in blocks:
                zz, yb = zmod(a), yhmod(b)

                @pl.when(yb // 2 == h)
                def _():
                    sib_copy(zz, yb).wait_recv()
                    total = acc[zz, yb % 2] + sib_in[zz, yb]

                    @pl.when(zz == q)
                    def _():
                        rs_own[yb % 2] = total

                    @pl.when(zz != q)
                    def _():
                        rs_out[zz, yb % 2] = total.astype(BF16)
                        rs_copy(zz, q, yb % 2).start()

    near = [0, 1, -1]
    for c in range(CHZ):
        z_step(1, c)
    z_step(2, 0)
    z_step(2, 1)
    y_step(1, 0)
    z_step(2, 2)
    z_step(2, 3)
    y_step(1, 1)
    for copy in local:
        copy.wait()
    gram([0, 1, -1], near)
    z_step(3, 0)
    z_step(3, 1)
    gram([2, -2], near)
    z_step(3, 2)
    z_step(3, 3)
    rs_step([1, -1, 0], near)
    gram([3, -3], near)
    rs_step([2, -2], near)
    y_step(2, 0)
    y_step(2, 1)
    gram([3, -3, 0, 1, -1, 2, -2], [2])
    rs_step([3, -3], near)
    rs_step([3, -3, 0, 1, -1, 2, -2], [2])
    for c in range(CHZ):
        z_step(4, c)
    gram([4], [0, 1, -1, 2])
    rs_step([4], [0, 1, -1, 2])
    for k in (2, 6, 1, 4, 3, 7, 5):
        for bit in range(2):
            rs_copy(q_of(k), q_of(k), bit).wait_recv()
    for bit in range(2):
        total = rs_own[bit]
        for k in range(1, 8):
            total = total + rs_in[q_of(k), bit].astype(F32)
        gram_own = total.astype(BF16)
        gb[x, y, :, bit * R : (bit + 1) * R] = gram_own
        ga[z, h, :, bit * R : (bit + 1) * R] = gram_own

    def xmod(d):
        return (x + d + NX) % NX

    bc, ac, bx, ax, gz, gs = {}, {}, {}, {}, {}, {}
    head, tail = pl.ds(0, HA), pl.ds(HA, R - HA)
    parts = {1: pl.ds(HA, 48), -1: pl.ds(HA + 48, R - HA - 48)}
    zhalf = {1: pl.ds(0, H), -1: pl.ds(H, H)}
    y_far = {1: device(y=ymod(2)), -1: device(y=ymod(-2))}
    z_far = {1: device(z=zmod(2)), -1: device(z=zmod(-2))}
    x_dev = {d: device(x=xmod(d)) for d in (1, -1, 2)}

    def b_cross(s, direct):
        held = gb.at[x, ymod(-s), tail]
        for d in (1, -1):
            bx[s, d] = send(held, held, x_dev[d])
        if direct:
            bx[s, 2] = send(held, held, x_dev[2])

    def b_relay(s):
        for d in (1, -1):
            bx[s, d].wait_recv()
            held = gb.at[xmod(-d), ymod(-s), parts[d]]
            bx[s, 2 * d] = send(held, held, x_dev[d])

    mine = gb.at[x, y, tail]
    for d in (1, -1):
        bc[d, 2] = send(mine, mine, y_far[d])
    mine = gb.at[x, y, head]
    for d in (1, -1, 2):
        ax[d] = send(mine, mine, x_dev[d])
    mine = gb.at[x, y, tail]
    for d in (1, -1):
        bc[d, 1] = send(mine, mine, y_dev[d])
    mine = ga.at[z, h]
    for d in (1, -1):
        gz[d, 2] = send(mine, mine, z_far[d])
    for d in (1, -1):
        gz[d, 1] = send(mine, mine, z_dev[d])
    b_cross(0, False)
    mine = gb.at[x, y, head]
    for d in (1, -1):
        ac[d, 1, 0] = send(mine, mine, y_dev[d])
    mine = ga.at[z, h]
    gs[0] = send(mine, mine, sibling)

    def b_step(s):
        for d in (1, -1):
            bc[d, s].wait_recv()
            if s == 2:
                held = gb.at[x, ymod(-2 * d), tail]
                bc[d, 3] = send(held, held, y_dev[d])
                held = gb.at[x, ymod(-2 * d), parts[d]]
                bc[d, 4] = send(held, held, y_far[d])
        for d in (1, -1) if s < 4 else (1,):
            b_cross(d * s, s > 2)

    def gz_step(s):
        for d in (1, -1):
            gz[d, s].wait_recv()
            if s == 2:
                held = ga.at[zmod(-2 * d), h]
                gz[d, 3] = send(held, held, z_dev[d])
                held = ga.at[zmod(-2 * d), h, zhalf[d]]
                gz[d, 4] = send(held, held, z_far[d])
        for d in (1, -1) if s < 4 else (1,):
            held = ga.at[zmod(-d * s), h]
            gs[d * s] = send(held, held, sibling)

    def a_step(s, rx):
        for d in (1, -1):
            if s == 0:
                if d == 1:
                    ax[rx].wait_recv()
            elif (d, s, rx) in ac:
                ac[d, s, rx].wait_recv()
            else:
                continue
            held = gb.at[xmod(-rx), ymod(-d * s), head]
            if s < 3:
                ac[d, s + 1, rx] = send(held, held, y_dev[d])
            if s == 2 and (rx in (0, 1)) == (d == 1):
                ac[d, 4, rx] = send(held, held, y_far[d])

    a_step(0, 1)
    a_step(0, -1)
    b_step(2)
    b_step(1)
    a_step(0, 2)
    b_relay(0)
    a_step(1, 0)
    gz_step(2)
    gz_step(1)
    a_step(1, 1)
    a_step(1, -1)
    b_step(3)
    b_step(4)
    a_step(1, 2)
    a_step(2, 0)
    b_relay(2)
    b_relay(-2)
    b_relay(1)
    b_relay(-1)
    a_step(2, 1)
    a_step(2, -1)
    gz_step(3)
    gz_step(4)
    a_step(2, 2)
    for s in (3, 4):
        for rx in (0, 1, -1, 2):
            a_step(s, rx)
    for copy in gs.values():
        copy.wait_recv()
    for (s, d), copy in bx.items():
        if abs(d) == 2 or abs(s) > 2:
            copy.wait_recv()

    def square(qq, total):
        xx, yy = qq // NYL, qq % NYL
        for half in range(2):
            right = jnp.concatenate(
                [gb[xx, 4 * half + yy], gb[xx, 4 * half + 2 + yy]], axis=0
            )
            total = total + jnp.dot(ga[qq, half], right, preferred_element_type=F32)
        return total

    total = jnp.zeros((R, W), F32)
    for qq in range(8):
        total = square(qq, total)
    poly = (quintic_b * gb[x, y].astype(F32) + quintic_c * total).astype(BF16)
    pb[q, h] = poly

    pc, ps = {}, {}
    for k in (2, 6, 1, 4, 3, 7, 5):
        pc[k] = send(pb.at[q, h], pb.at[q, h], q_dev(k))
    ps[0] = send(pb.at[q, h], pb.at[q, h], sibling)

    drain_at = len(pending) - 8
    for copy in pending[:drain_at]:
        copy.wait_send()
    del pending[:drain_at]
    for k in range(1, 8):
        for bit in range(2):
            rs_copy(q_of(k), q, bit).wait_send()
    for zz in range(NZ):
        for bit in range(2):
            sib_copy(zz, 2 * (1 - h) + bit).wait_send()

    def turn(qq, half):
        turned = pb[qq, half].astype(F32).T.astype(BF16)
        columns = pl.ds(pl.multiple_of(qq * R, R), R)
        for part in range(2):
            pt[2 * half + part, :, columns] = turned[part * R : (part + 1) * R]

    turn(q, h)

    def from_q(k):
        dx, dy = k // 2, k % 2
        return ((x - dx + NX) % NX) * NYL + (yl + dy) % NYL

    for k in (2, 6, 1, 4, 3, 7, 5):
        held = pb.at[from_q(k), h]
        pc[k].wait_recv()
        ps[k] = send(held, held, sibling)
        turn(from_q(k), h)
    for k in (0, 2, 6, 1, 4, 3, 7, 5):
        ps[k].wait_recv()
        turn(from_q(k), 1 - h)

    zr, yr = {}, {}

    def z_part(offsets):
        value = 0.0
        for half in range(2):
            left = jnp.concatenate([pb[zmod(a), half] for a in offsets], axis=0)
            right = xj[2 * half : 2 * half + 2, :, 0:CZ].reshape(W, CZ)
            value = value + jnp.dot(left, right, preferred_element_type=F32)
        for n, a in enumerate(offsets):
            zp[a % NZ] = value[n * R : (n + 1) * R]

    def y_part(offsets):
        left = jnp.concatenate([pt[yhmod(a)] for a in offsets], axis=0)
        right = xi[:, :, CZ:C].reshape(NZ * R, CY)
        value = jnp.dot(left, right, preferred_element_type=F32)
        for n, a in enumerate(offsets):
            yp[a % NYH] = value[n * R : (n + 1) * R]

    def first(d):
        return 0 if d == 1 else 1

    def z_send(d, s, c):
        n = 0 if d == 1 else 1
        value = zp[(d * (4 - s)) % NZ, halves[c]]
        for before in {2: (1, 0), 3: (2,)}.get(s, ()):
            if (d, before, c) in zr:
                zr[d, before, c].wait_recv()
                value = value + zs_in[n, before, halves[c]].astype(F32)
        zs_out[n, s, halves[c]] = value.astype(BF16)
        to = z_dev[d] if s else z_far[d]
        zr[d, s, c] = send(zs_out.at[n, s, halves[c]], zs_in.at[n, s, halves[c]], to)

    def y_send(d, s, c):
        n = 0 if d == 1 else 1
        value = yp[(d * (2 - s)) % NYH, halves[c]]
        if (d, s - 1, c) in yr:
            yr[d, s - 1, c].wait_recv()
            value = value + ys_in[n, s - 1, halves[c]].astype(F32)
        ys_out[n, s, halves[c]] = value.astype(BF16)
        yr[d, s, c] = send(ys_out.at[n, s, halves[c]], ys_in.at[n, s, halves[c]], yh_dev[d])

    def z_got(d, s, c):
        zr[d, s, c].wait_recv()
        return zs_in[0 if d == 1 else 1, s, halves[c]].astype(F32)

    def y_got(d, s, c):
        yr[d, s, c].wait_recv()
        return ys_in[0 if d == 1 else 1, s, halves[c]].astype(F32)

    z_part([4])
    for d in (1, -1):
        z_send(d, 0, first(d))
    y_part([2])
    for d in (1, -1):
        y_send(d, 0, first(d))
    z_part([3, -3])
    for c in (0, 1):
        for d in (1, -1):
            z_send(d, 1, first(d) if c == 0 else 1 - first(d))
    y_part([1, -1])
    for d in (1, -1):
        y_send(d, 1, 1 - first(d))
    z_part([2, -2])
    z_part([1, -1])
    for d in (1, -1):
        z_send(d, 2, first(d))
    for d in (1, -1):
        z_send(d, 2, 1 - first(d))
    for d in (1, -1):
        y_send(d, 1, first(d))
    y_part([0])
    z_part([0])
    for d in (1, -1):
        z_send(d, 3, first(d))
    for d in (1, -1):
        z_send(d, 3, 1 - first(d))
    scale = math.sqrt(max(M, N))
    for c in (0, 1):
        rows = halves[c]
        value = yp[0, rows] + y_got(1, 1, c) + y_got(-1, 1, c)
        out_ref[rows, CZ:C] = scale * (quintic_a * xi[z, rows, CZ:C].astype(F32) + value)
    for c in (0, 1):
        rows = halves[c]
        value = zp[0, rows] + z_got(1, 3, c) + z_got(-1, 3, c)
        out_ref[rows, 0:CZ] = scale * (quintic_a * xi[z, rows, 0:CZ].astype(F32) + value)

    for copy in pending:
        copy.wait_send()


def per_device(momentum):
    return pl.pallas_call(
        kernel,
        out_shape=jax.ShapeDtypeStruct((R, C), F32),
        in_specs=[pl.BlockSpec(memory_space=pl.ANY)],
        out_specs=pl.BlockSpec(memory_space=pltpu.VMEM),
        scratch_shapes=[
            pltpu.VMEM((NZ, R, C), BF16),
            pltpu.VMEM((NYH, R, C), BF16),
            pltpu.VMEM((NZ, 2, R, R), F32),
            pltpu.VMEM((NZ, NYH, R, R), F32),
            pltpu.VMEM((NZ, NYH, R, R), F32),
            pltpu.VMEM((2, R, R), F32),
            pltpu.VMEM((NZ, 2, R, R), BF16),
            pltpu.VMEM((NZ, 2, R, R), BF16),
            pltpu.VMEM((NZ, 2, R, W), BF16),
            pltpu.VMEM((NX, NY, R, W), BF16),
            pltpu.VMEM((NZ, 2, R, W), BF16),
            pltpu.VMEM((NYH, R, NZ * R), BF16),
            pltpu.VMEM((2, 4, R, CZ), BF16),
            pltpu.VMEM((2, 4, R, CZ), BF16),
            pltpu.VMEM((2, 2, R, CY), BF16),
            pltpu.VMEM((2, 2, R, CY), BF16),
            pltpu.VMEM((NZ, R, CZ), F32),
            pltpu.VMEM((NYH, R, CY), F32),
            pltpu.SemaphoreType.DMA((SEMS,)),
            pltpu.SemaphoreType.DMA((SEMS,)),
            pltpu.SemaphoreType.DMA((NZ, 2)),
            pltpu.SemaphoreType.DMA((NZ, 2)),
            pltpu.SemaphoreType.DMA((NZ, NYH)),
            pltpu.SemaphoreType.DMA((NZ, NYH)),
            pltpu.SemaphoreType.DMA((2,)),
        ],
        compiler_params=pltpu.CompilerParams(
            collective_id=0, has_side_effects=True, vmem_limit_bytes=60 * 1024 * 1024
        ),
        cost_estimate=pl.CostEstimate(flops=2200000000, bytes_accessed=1000000, transcendentals=0),
        name="newton_schulz",
    )(momentum)


def solution(mesh):
    return jax.shard_map(
        per_device, mesh=mesh, in_specs=(P("row", "col"),), out_specs=P("row", "col"), check_vma=False
    )
```

```python
import math

import jax
import jax.numpy as jnp
from jax import lax
from jax.experimental import pallas as pl
from jax.experimental.pallas import tpu as pltpu
from jax.sharding import PartitionSpec as P

M = 4096
N = 14336
quintic_a = 3.4445
quintic_b = -4.775
quintic_c = 2.0315

NZ, NYH, NX, NYL = 8, 4, 4, 2
NY = NYH * NYL
R = 128
C = 896
H = R // 2
W = 256
CZ = 384
CY = C - CZ
SEMS = 230
CHZ = 4
CHY = 2
HA = 48

F32 = jnp.float32
BF16 = jnp.bfloat16


def kernel(
    x_ref, out_ref,
    xi, xj, acc, sib_out, sib_in, rs_own, rs_out, rs_in, ga, gb, pb, pt,
    zs_out, zs_in, ys_out, ys_in, zp, yp,
    send_sems, recv_sems, rs_send, rs_recv, sib_send, sib_recv, local_sems,
):
    row = lax.axis_index("row")
    col = lax.axis_index("col")
    z, yh = row // NYH, row % NYH
    q, h = col // 2, col % 2
    x, yl = q // NYL, q % NYL
    y = yh * NYL + yl

    def device(z=z, y=y, x=x, h=h):
        return (z * NYH + y // NYL, (x * NYL + y % NYL) * 2 + h)

    def zmod(d):
        return (z + d + NZ) % NZ

    def ymod(d):
        return (y + d + NY) % NY

    def yhmod(d):
        return (yh + d + NYH) % NYH

    z_dev = {1: device(z=zmod(1)), -1: device(z=zmod(-1))}
    y_dev = {1: device(y=ymod(1)), -1: device(y=ymod(-1))}
    yh_dev = {1: device(y=ymod(2)), -1: device(y=ymod(-2))}
    sibling = device(h=1 - h)

    def q_dev(k):
        dx, dy = k // 2, k % 2
        return device(x=(x + dx) % NX, y=yh * NYL + (yl + dy) % NYL)

    def q_of(k):
        dx, dy = k // 2, k % 2
        return ((x + dx) % NX) * NYL + (yl + dy) % NYL

    pending = []
    count = [0]

    def send(src, dst, to):
        n = count[0]
        count[0] += 1
        copy = pltpu.make_async_remote_copy(
            src_ref=src, dst_ref=dst, send_sem=send_sems.at[n], recv_sem=recv_sems.at[n],
            device_id=to, device_id_type=pl.DeviceIdType.MESH,
        )
        copy.start()
        pending.append(copy)
        return copy

    barrier = pltpu.get_barrier_semaphore()
    partners = [z_dev[1], z_dev[-1], yh_dev[1], yh_dev[-1], y_dev[1], y_dev[-1], sibling]
    partners += [q_dev(k) for k in range(1, 8)] + [device(z=zmod(2)), device(z=zmod(-2))]
    for partner in partners:
        pl.semaphore_signal(barrier, inc=1, device_id=partner, device_id_type=pl.DeviceIdType.MESH)
    pl.semaphore_wait(barrier, len(partners))

    top, low = pl.ds(0, H), pl.ds(H, H)
    halves = (top, low)
    cz = [pl.ds(c * R // CHZ, R // CHZ) for c in range(CHZ)]
    cy = [pl.ds(c * R // CHY, R // CHY) for c in range(CHY)]
    zc, yc = {}, {}
    for c in range(max(CHZ, CHY)):
        for d in (1, -1):
            if c < CHZ:
                zc[d, 1, c] = send(x_ref.at[cz[c]], xi.at[z, cz[c]], z_dev[d])
        for d in (1, -1):
            if c < CHY:
                yc[d, 1, c] = send(x_ref.at[cy[c]], xj.at[yh, cy[c]], yh_dev[d])
    local = [
        pltpu.make_async_copy(x_ref, xi.at[z], local_sems.at[0]),
        pltpu.make_async_copy(x_ref, xj.at[yh], local_sems.at[1]),
    ]
    for copy in local:
        copy.start()

    def z_step(s, c):
        for d in (1, -1):
            if (d, s, c) not in zc:
                continue
            zc[d, s, c].wait_recv()
            if s < 3 or (s == 3 and (2 * c < CHZ) == (d == 1)):
                held = xi.at[zmod(-d * s), cz[c]]
                zc[d, s + 1, c] = send(held, held, z_dev[d])

    def y_step(s, c):
        for d in (1, -1):
            if (d, s, c) not in yc:
                continue
            yc[d, s, c].wait_recv()
            if s == 1 and (2 * c < CHY) == (d == 1):
                held = xj.at[yhmod(-d), cy[c]]
                yc[d, 2, c] = send(held, held, yh_dev[d])

    def sib_copy(zz, yb):
        return pltpu.make_async_remote_copy(
            src_ref=sib_out.at[zz, yb], dst_ref=sib_in.at[zz, yb],
            send_sem=sib_send.at[zz, yb], recv_sem=sib_recv.at[zz, yb],
            device_id=sibling, device_id_type=pl.DeviceIdType.MESH,
        )

    def rs_copy(to, slot, bit):
        return pltpu.make_async_remote_copy(
            src_ref=rs_out.at[to, bit], dst_ref=rs_in.at[slot, bit],
            send_sem=rs_send.at[to, bit], recv_sem=rs_recv.at[slot, bit],
            device_id=device(x=to // NYL, y=yh * NYL + to % NYL),
            device_id_type=pl.DeviceIdType.MESH,
        )

    def gram(offsets, blocks):
        left = jnp.concatenate([xi[zmod(a)] for a in offsets], axis=0)
        right = jnp.concatenate([xj[yhmod(b)] for b in blocks], axis=0)
        value = lax.dot_general(left, right, (((1,), (1,)), ((), ())), preferred_element_type=F32)
        for n, a in enumerate(offsets):
            for m, b in enumerate(blocks):
                part = value[n * R : (n + 1) * R, m * R : (m + 1) * R]
                zz, yb = zmod(a), yhmod(b)

                @pl.when(yb // 2 == h)
                def _():
                    acc[zz, yb % 2] = part

                @pl.when(yb // 2 != h)
                def _():
                    sib_out[zz, yb] = part
                    sib_copy(zz, yb).start()

    def rs_step(offsets, blocks):
        for a in offsets:
            for b in blocks:
                zz, yb = zmod(a), yhmod(b)

                @pl.when(yb // 2 == h)
                def _():
                    sib_copy(zz, yb).wait_recv()
                    total = acc[zz, yb % 2] + sib_in[zz, yb]

                    @pl.when(zz == q)
                    def _():
                        rs_own[yb % 2] = total

                    @pl.when(zz != q)
                    def _():
                        rs_out[zz, yb % 2] = total.astype(BF16)
                        rs_copy(zz, q, yb % 2).start()

    near = [0, 1, -1]
    for c in range(CHZ):
        z_step(1, c)
    z_step(2, 0)
    z_step(2, 1)
    y_step(1, 0)
    z_step(2, 2)
    z_step(2, 3)
    y_step(1, 1)
    for copy in local:
        copy.wait()
    gram([0, 1, -1], near)
    z_step(3, 0)
    z_step(3, 1)
    gram([2, -2], near)
    z_step(3, 2)
    z_step(3, 3)
    rs_step([1, -1, 0], near)
    gram([3, -3], near)
    rs_step([2, -2], near)
    for c in (0, 2, 1, 3):
        z_step(4, c)
    gram([4], near)
    rs_step([3, -3], near)
    y_step(2, 0)
    y_step(2, 1)
    gram([4, 3, -3, 0, 1, -1, 2, -2], [2])
    rs_step([4], near)
    rs_step([4, 3, -3, 0, 1, -1, 2, -2], [2])
    for k in (2, 6, 1, 4, 3, 7, 5):
        for bit in range(2):
            rs_copy(q_of(k), q_of(k), bit).wait_recv()
    for bit in range(2):
        total = rs_own[bit]
        for k in range(1, 8):
            total = total + rs_in[q_of(k), bit].astype(F32)
        gram_own = total.astype(BF16)
        gb[x, y, :, bit * R : (bit + 1) * R] = gram_own
        ga[z, h, :, bit * R : (bit + 1) * R] = gram_own

    def xmod(d):
        return (x + d + NX) % NX

    bc, ac, bx, ax, gz, gs = {}, {}, {}, {}, {}, {}
    head, tail = pl.ds(0, HA), pl.ds(HA, R - HA)
    parts = {1: pl.ds(HA, 48), -1: pl.ds(HA + 48, R - HA - 48)}
    zhalf = {1: pl.ds(0, H), -1: pl.ds(H, H)}
    y_far = {1: device(y=ymod(2)), -1: device(y=ymod(-2))}
    z_far = {1: device(z=zmod(2)), -1: device(z=zmod(-2))}
    x_dev = {d: device(x=xmod(d)) for d in (1, -1, 2)}

    def b_cross(s, direct):
        held = gb.at[x, ymod(-s), tail]
        for d in (1, -1):
            bx[s, d] = send(held, held, x_dev[d])
        if direct:
            bx[s, 2] = send(held, held, x_dev[2])

    def b_relay(s):
        for d in (1, -1):
            bx[s, d].wait_recv()
            held = gb.at[xmod(-d), ymod(-s), parts[d]]
            bx[s, 2 * d] = send(held, held, x_dev[d])

    mine = gb.at[x, y, tail]
    for d in (1, -1):
        bc[d, 2] = send(mine, mine, y_far[d])
    mine = gb.at[x, y, head]
    for d in (1, -1, 2):
        ax[d] = send(mine, mine, x_dev[d])
    mine = gb.at[x, y, tail]
    for d in (1, -1):
        bc[d, 1] = send(mine, mine, y_dev[d])
    mine = ga.at[z, h]
    for d in (1, -1):
        gz[d, 2] = send(mine, mine, z_far[d])
    for d in (1, -1):
        gz[d, 1] = send(mine, mine, z_dev[d])
    b_cross(0, False)
    mine = gb.at[x, y, head]
    for d in (1, -1):
        ac[d, 1, 0] = send(mine, mine, y_dev[d])
    mine = ga.at[z, h]
    gs[0] = send(mine, mine, sibling)

    def b_step(s):
        for d in (1, -1):
            bc[d, s].wait_recv()
            if s == 2:
                held = gb.at[x, ymod(-2 * d), tail]
                bc[d, 3] = send(held, held, y_dev[d])
                held = gb.at[x, ymod(-2 * d), parts[d]]
                bc[d, 4] = send(held, held, y_far[d])
        for d in (1, -1) if s < 4 else (1,):
            b_cross(d * s, s > 2)

    def gz_step(s):
        for d in (1, -1):
            gz[d, s].wait_recv()
            if s == 2:
                held = ga.at[zmod(-2 * d), h]
                gz[d, 3] = send(held, held, z_dev[d])
                held = ga.at[zmod(-2 * d), h, zhalf[d]]
                gz[d, 4] = send(held, held, z_far[d])
        for d in (1, -1) if s < 4 else (1,):
            held = ga.at[zmod(-d * s), h]
            gs[d * s] = send(held, held, sibling)

    def a_step(s, rx):
        for d in (1, -1):
            if s == 0:
                if d == 1:
                    ax[rx].wait_recv()
            elif (d, s, rx) in ac:
                ac[d, s, rx].wait_recv()
            else:
                continue
            held = gb.at[xmod(-rx), ymod(-d * s), head]
            if s < 3:
                ac[d, s + 1, rx] = send(held, held, y_dev[d])
            if s == 2 and (rx in (0, 1)) == (d == 1):
                ac[d, 4, rx] = send(held, held, y_far[d])

    a_step(0, 1)
    a_step(0, -1)
    b_step(2)
    b_step(1)
    a_step(0, 2)
    b_relay(0)
    a_step(1, 0)
    gz_step(2)
    gz_step(1)
    a_step(1, 1)
    a_step(1, -1)
    b_step(3)
    b_step(4)
    a_step(1, 2)
    a_step(2, 0)
    a_step(2, 1)
    a_step(2, -1)
    b_relay(1)
    b_relay(-1)
    b_relay(2)
    b_relay(-2)
    a_step(2, 2)
    gz_step(3)
    gz_step(4)
    for s in (3, 4):
        for rx in (0, 1, -1, 2):
            a_step(s, rx)
    for copy in gs.values():
        copy.wait_recv()
    for (s, d), copy in bx.items():
        if abs(d) == 2 or abs(s) > 2:
            copy.wait_recv()

    def square(qq, total):
        xx, yy = qq // NYL, qq % NYL
        for half in range(2):
            right = jnp.concatenate(
                [gb[xx, 4 * half + yy], gb[xx, 4 * half + 2 + yy]], axis=0
            )
            total = total + jnp.dot(ga[qq, half], right, preferred_element_type=F32)
        return total

    total = jnp.zeros((R, W), F32)
    for qq in range(8):
        total = square(qq, total)
    poly = (quintic_b * gb[x, y].astype(F32) + quintic_c * total).astype(BF16)
    pb[q, h] = poly

    pc, ps = {}, {}
    for k in (2, 6, 1, 4, 3, 7, 5):
        pc[k] = send(pb.at[q, h], pb.at[q, h], q_dev(k))
    ps[0] = send(pb.at[q, h], pb.at[q, h], sibling)

    drain_at = len(pending) - 8
    for copy in pending[:drain_at]:
        copy.wait_send()
    del pending[:drain_at]
    for k in range(1, 8):
        for bit in range(2):
            rs_copy(q_of(k), q, bit).wait_send()
    for zz in range(NZ):
        for bit in range(2):
            sib_copy(zz, 2 * (1 - h) + bit).wait_send()

    def turn(qq, half):
        turned = pb[qq, half].astype(F32).T.astype(BF16)
        columns = pl.ds(pl.multiple_of(qq * R, R), R)
        for part in range(2):
            pt[2 * half + part, :, columns] = turned[part * R : (part + 1) * R]

    turn(q, h)

    def from_q(k):
        dx, dy = k // 2, k % 2
        return ((x - dx + NX) % NX) * NYL + (yl + dy) % NYL

    for k in (2, 6, 1, 4, 3, 7, 5):
        held = pb.at[from_q(k), h]
        pc[k].wait_recv()
        ps[k] = send(held, held, sibling)
        turn(from_q(k), h)
    for k in (0, 2, 6, 1, 4, 3, 7, 5):
        ps[k].wait_recv()
        turn(from_q(k), 1 - h)

    zr, yr = {}, {}

    def z_part(offsets):
        value = 0.0
        for half in range(2):
            left = jnp.concatenate([pb[zmod(a), half] for a in offsets], axis=0)
            right = xj[2 * half : 2 * half + 2, :, 0:CZ].reshape(W, CZ)
            value = value + jnp.dot(left, right, preferred_element_type=F32)
        for n, a in enumerate(offsets):
            zp[a % NZ] = value[n * R : (n + 1) * R]

    def y_part(offsets):
        left = jnp.concatenate([pt[yhmod(a)] for a in offsets], axis=0)
        right = xi[:, :, CZ:C].reshape(NZ * R, CY)
        value = jnp.dot(left, right, preferred_element_type=F32)
        for n, a in enumerate(offsets):
            yp[a % NYH] = value[n * R : (n + 1) * R]

    def first(d):
        return 0 if d == 1 else 1

    def z_send(d, s, c):
        n = 0 if d == 1 else 1
        value = zp[(d * (4 - s)) % NZ, halves[c]]
        for before in {2: (1, 0), 3: (2,)}.get(s, ()):
            if (d, before, c) in zr:
                zr[d, before, c].wait_recv()
                value = value + zs_in[n, before, halves[c]].astype(F32)
        zs_out[n, s, halves[c]] = value.astype(BF16)
        to = z_dev[d] if s else z_far[d]
        zr[d, s, c] = send(zs_out.at[n, s, halves[c]], zs_in.at[n, s, halves[c]], to)

    def y_send(d, s, c):
        n = 0 if d == 1 else 1
        value = yp[(d * (2 - s)) % NYH, halves[c]]
        if (d, s - 1, c) in yr:
            yr[d, s - 1, c].wait_recv()
            value = value + ys_in[n, s - 1, halves[c]].astype(F32)
        ys_out[n, s, halves[c]] = value.astype(BF16)
        yr[d, s, c] = send(ys_out.at[n, s, halves[c]], ys_in.at[n, s, halves[c]], yh_dev[d])

    def z_got(d, s, c):
        zr[d, s, c].wait_recv()
        return zs_in[0 if d == 1 else 1, s, halves[c]].astype(F32)

    def y_got(d, s, c):
        yr[d, s, c].wait_recv()
        return ys_in[0 if d == 1 else 1, s, halves[c]].astype(F32)

    z_part([4])
    for d in (1, -1):
        z_send(d, 0, first(d))
    y_part([2])
    for d in (1, -1):
        y_send(d, 0, first(d))
    z_part([3, -3])
    for c in (0, 1):
        for d in (1, -1):
            z_send(d, 1, first(d) if c == 0 else 1 - first(d))
    y_part([1, -1])
    for d in (1, -1):
        y_send(d, 1, 1 - first(d))
    z_part([2, -2])
    z_part([1, -1])
    for d in (1, -1):
        z_send(d, 2, first(d))
    for d in (1, -1):
        z_send(d, 2, 1 - first(d))
    for d in (1, -1):
        y_send(d, 1, first(d))
    y_part([0])
    z_part([0])
    for d in (1, -1):
        z_send(d, 3, first(d))
    for d in (1, -1):
        z_send(d, 3, 1 - first(d))
    scale = math.sqrt(max(M, N))
    for c in (0, 1):
        rows = halves[c]
        value = yp[0, rows] + y_got(1, 1, c) + y_got(-1, 1, c)
        out_ref[rows, CZ:C] = scale * (quintic_a * xi[z, rows, CZ:C].astype(F32) + value)
    for c in (0, 1):
        rows = halves[c]
        value = zp[0, rows] + z_got(1, 3, c) + z_got(-1, 3, c)
        out_ref[rows, 0:CZ] = scale * (quintic_a * xi[z, rows, 0:CZ].astype(F32) + value)

    for copy in pending:
        copy.wait_send()


def per_device(momentum):
    return pl.pallas_call(
        kernel,
        out_shape=jax.ShapeDtypeStruct((R, C), F32),
        in_specs=[pl.BlockSpec(memory_space=pl.ANY)],
        out_specs=pl.BlockSpec(memory_space=pltpu.VMEM),
        scratch_shapes=[
            pltpu.VMEM((NZ, R, C), BF16),
            pltpu.VMEM((NYH, R, C), BF16),
            pltpu.VMEM((NZ, 2, R, R), F32),
            pltpu.VMEM((NZ, NYH, R, R), F32),
            pltpu.VMEM((NZ, NYH, R, R), F32),
            pltpu.VMEM((2, R, R), F32),
            pltpu.VMEM((NZ, 2, R, R), BF16),
            pltpu.VMEM((NZ, 2, R, R), BF16),
            pltpu.VMEM((NZ, 2, R, W), BF16),
            pltpu.VMEM((NX, NY, R, W), BF16),
            pltpu.VMEM((NZ, 2, R, W), BF16),
            pltpu.VMEM((NYH, R, NZ * R), BF16),
            pltpu.VMEM((2, 4, R, CZ), BF16),
            pltpu.VMEM((2, 4, R, CZ), BF16),
            pltpu.VMEM((2, 2, R, CY), BF16),
            pltpu.VMEM((2, 2, R, CY), BF16),
            pltpu.VMEM((NZ, R, CZ), F32),
            pltpu.VMEM((NYH, R, CY), F32),
            pltpu.SemaphoreType.DMA((SEMS,)),
            pltpu.SemaphoreType.DMA((SEMS,)),
            pltpu.SemaphoreType.DMA((NZ, 2)),
            pltpu.SemaphoreType.DMA((NZ, 2)),
            pltpu.SemaphoreType.DMA((NZ, NYH)),
            pltpu.SemaphoreType.DMA((NZ, NYH)),
            pltpu.SemaphoreType.DMA((2,)),
        ],
        compiler_params=pltpu.CompilerParams(
            collective_id=0, has_side_effects=True, vmem_limit_bytes=48 * 1024 * 1024
        ),
        cost_estimate=pl.CostEstimate(flops=2200000000, bytes_accessed=1000000, transcendentals=0),
        name="newton_schulz",
    )(momentum)


def solution(mesh):
    return jax.shard_map(
        per_device, mesh=mesh, in_specs=(P("row", "col"),), out_specs=P("row", "col"), check_vma=False
    )
```

```python
import math

import jax
import jax.numpy as jnp
from jax import lax
from jax.experimental import pallas as pl
from jax.experimental.pallas import tpu as pltpu
from jax.sharding import PartitionSpec as P

M = 4096
N = 14336
quintic_a = 3.4445
quintic_b = -4.775
quintic_c = 2.0315

NZ, NYH, NX, NYL = 8, 4, 4, 2
NY = NYH * NYL
R = 128
C = 896
H = R // 2
W = 256
CZ = 384
CY = C - CZ
SEMS = 230
CHZ = 4
CHY = 2
HA = 48

F32 = jnp.float32
BF16 = jnp.bfloat16


def kernel(
    x_ref, out_ref,
    xi, xj, acc, sib_out, sib_in, rs_own, rs_out, rs_in, ga, gb, pb, pt,
    zs_out, zs_in, ys_out, ys_in, zp, yp,
    send_sems, recv_sems, rs_send, rs_recv, sib_send, sib_recv, local_sems,
):
    row = lax.axis_index("row")
    col = lax.axis_index("col")
    z, yh = row // NYH, row % NYH
    q, h = col // 2, col % 2
    x, yl = q // NYL, q % NYL
    y = yh * NYL + yl

    def device(z=z, y=y, x=x, h=h):
        return (z * NYH + y // NYL, (x * NYL + y % NYL) * 2 + h)

    def zmod(d):
        return (z + d + NZ) % NZ

    def ymod(d):
        return (y + d + NY) % NY

    def yhmod(d):
        return (yh + d + NYH) % NYH

    z_dev = {1: device(z=zmod(1)), -1: device(z=zmod(-1))}
    y_dev = {1: device(y=ymod(1)), -1: device(y=ymod(-1))}
    yh_dev = {1: device(y=ymod(2)), -1: device(y=ymod(-2))}
    sibling = device(h=1 - h)

    def q_dev(k):
        dx, dy = k // 2, k % 2
        return device(x=(x + dx) % NX, y=yh * NYL + (yl + dy) % NYL)

    def q_of(k):
        dx, dy = k // 2, k % 2
        return ((x + dx) % NX) * NYL + (yl + dy) % NYL

    pending = []
    count = [0]

    def send(src, dst, to):
        n = count[0]
        count[0] += 1
        copy = pltpu.make_async_remote_copy(
            src_ref=src, dst_ref=dst, send_sem=send_sems.at[n], recv_sem=recv_sems.at[n],
            device_id=to, device_id_type=pl.DeviceIdType.MESH,
        )
        copy.start()
        pending.append(copy)
        return copy

    barrier = pltpu.get_barrier_semaphore()
    partners = [z_dev[1], z_dev[-1], yh_dev[1], yh_dev[-1], y_dev[1], y_dev[-1], sibling]
    partners += [q_dev(k) for k in range(1, 8)] + [device(z=zmod(2)), device(z=zmod(-2))]
    for partner in partners:
        pl.semaphore_signal(barrier, inc=1, device_id=partner, device_id_type=pl.DeviceIdType.MESH)
    pl.semaphore_wait(barrier, len(partners))

    top, low = pl.ds(0, H), pl.ds(H, H)
    halves = (top, low)
    cz = [pl.ds(c * R // CHZ, R // CHZ) for c in range(CHZ)]
    cy = [pl.ds(c * R // CHY, R // CHY) for c in range(CHY)]
    zc, yc = {}, {}
    for c in range(max(CHZ, CHY)):
        for d in (1, -1):
            if c < CHZ:
                zc[d, 1, c] = send(x_ref.at[cz[c]], xi.at[z, cz[c]], z_dev[d])
        for d in (1, -1):
            if c < CHY:
                yc[d, 1, c] = send(x_ref.at[cy[c]], xj.at[yh, cy[c]], yh_dev[d])
    local = [
        pltpu.make_async_copy(x_ref, xi.at[z], local_sems.at[0]),
        pltpu.make_async_copy(x_ref, xj.at[yh], local_sems.at[1]),
    ]
    for copy in local:
        copy.start()

    def z_step(s, c):
        for d in (1, -1):
            if (d, s, c) not in zc:
                continue
            zc[d, s, c].wait_recv()
            if s < 3 or (s == 3 and (2 * c < CHZ) == (d == 1)):
                held = xi.at[zmod(-d * s), cz[c]]
                zc[d, s + 1, c] = send(held, held, z_dev[d])

    def y_step(s, c):
        for d in (1, -1):
            if (d, s, c) not in yc:
                continue
            yc[d, s, c].wait_recv()
            if s == 1 and (2 * c < CHY) == (d == 1):
                held = xj.at[yhmod(-d), cy[c]]
                yc[d, 2, c] = send(held, held, yh_dev[d])

    def sib_copy(zz, yb):
        return pltpu.make_async_remote_copy(
            src_ref=sib_out.at[zz, yb], dst_ref=sib_in.at[zz, yb],
            send_sem=sib_send.at[zz, yb], recv_sem=sib_recv.at[zz, yb],
            device_id=sibling, device_id_type=pl.DeviceIdType.MESH,
        )

    def rs_copy(to, slot, bit):
        return pltpu.make_async_remote_copy(
            src_ref=rs_out.at[to, bit], dst_ref=rs_in.at[slot, bit],
            send_sem=rs_send.at[to, bit], recv_sem=rs_recv.at[slot, bit],
            device_id=device(x=to // NYL, y=yh * NYL + to % NYL),
            device_id_type=pl.DeviceIdType.MESH,
        )

    def gram(offsets, blocks):
        left = jnp.concatenate([xi[zmod(a)] for a in offsets], axis=0)
        right = jnp.concatenate([xj[yhmod(b)] for b in blocks], axis=0)
        value = lax.dot_general(left, right, (((1,), (1,)), ((), ())), preferred_element_type=F32)
        for n, a in enumerate(offsets):
            for m, b in enumerate(blocks):
                part = value[n * R : (n + 1) * R, m * R : (m + 1) * R]
                zz, yb = zmod(a), yhmod(b)

                @pl.when(yb // 2 == h)
                def _():
                    acc[zz, yb % 2] = part

                @pl.when(yb // 2 != h)
                def _():
                    sib_out[zz, yb] = part
                    sib_copy(zz, yb).start()

    def rs_step(offsets, blocks):
        for a in offsets:
            for b in blocks:
                zz, yb = zmod(a), yhmod(b)

                @pl.when(yb // 2 == h)
                def _():
                    sib_copy(zz, yb).wait_recv()
                    total = acc[zz, yb % 2] + sib_in[zz, yb]

                    @pl.when(zz == q)
                    def _():
                        rs_own[yb % 2] = total

                    @pl.when(zz != q)
                    def _():
                        rs_out[zz, yb % 2] = total.astype(BF16)
                        rs_copy(zz, q, yb % 2).start()

    near = [0, 1, -1]
    for c in range(CHZ):
        z_step(1, c)
    z_step(2, 0)
    z_step(2, 1)
    y_step(1, 0)
    z_step(2, 2)
    z_step(2, 3)
    y_step(1, 1)
    for copy in local:
        copy.wait()
    gram([0, 1, -1], near)
    z_step(3, 0)
    z_step(3, 1)
    gram([2, -2], near)
    z_step(3, 2)
    z_step(3, 3)
    rs_step([1, -1, 0], near)
    gram([3, -3], near)
    rs_step([2, -2], near)
    for c in (0, 2, 1, 3):
        z_step(4, c)
    gram([4], near)
    rs_step([3, -3], near)
    y_step(2, 0)
    y_step(2, 1)
    gram([4, 3, -3, 0, 1, -1, 2, -2], [2])
    rs_step([4], near)
    rs_step([4, 3, -3, 0, 1, -1, 2, -2], [2])
    for k in (2, 6, 1, 4, 3, 7, 5):
        for bit in range(2):
            rs_copy(q_of(k), q_of(k), bit).wait_recv()
    for bit in range(2):
        total = rs_own[bit]
        for k in range(1, 8):
            total = total + rs_in[q_of(k), bit].astype(F32)
        gram_own = total.astype(BF16)
        gb[x, y, :, bit * R : (bit + 1) * R] = gram_own
        ga[z, h, :, bit * R : (bit + 1) * R] = gram_own

    def xmod(d):
        return (x + d + NX) % NX

    bc, ac, bx, ax, gz, gs = {}, {}, {}, {}, {}, {}
    head, tail = pl.ds(0, HA), pl.ds(HA, R - HA)
    parts = {1: pl.ds(HA, 48), -1: pl.ds(HA + 48, R - HA - 48)}
    zhalf = {1: pl.ds(0, H), -1: pl.ds(H, H)}
    y_far = {1: device(y=ymod(2)), -1: device(y=ymod(-2))}
    z_far = {1: device(z=zmod(2)), -1: device(z=zmod(-2))}
    x_dev = {d: device(x=xmod(d)) for d in (1, -1, 2)}

    def b_cross(s, direct):
        held = gb.at[x, ymod(-s), tail]
        for d in (1, -1):
            bx[s, d] = send(held, held, x_dev[d])
        if direct:
            bx[s, 2] = send(held, held, x_dev[2])

    def b_relay(s):
        for d in (1, -1):
            bx[s, d].wait_recv()
            held = gb.at[xmod(-d), ymod(-s), parts[d]]
            bx[s, 2 * d] = send(held, held, x_dev[d])

    mine = gb.at[x, y, tail]
    for d in (1, -1):
        bc[d, 2] = send(mine, mine, y_far[d])
    mine = gb.at[x, y, head]
    for d in (1, -1, 2):
        ax[d] = send(mine, mine, x_dev[d])
    mine = gb.at[x, y, tail]
    for d in (1, -1):
        bc[d, 1] = send(mine, mine, y_dev[d])
    mine = ga.at[z, h]
    for d in (1, -1):
        gz[d, 2] = send(mine, mine, z_far[d])
    for d in (1, -1):
        gz[d, 1] = send(mine, mine, z_dev[d])
    b_cross(0, True)
    mine = gb.at[x, y, head]
    for d in (1, -1):
        ac[d, 1, 0] = send(mine, mine, y_dev[d])
    mine = ga.at[z, h]
    gs[0] = send(mine, mine, sibling)

    def b_step(s):
        for d in (1, -1):
            bc[d, s].wait_recv()
            if s == 2:
                held = gb.at[x, ymod(-2 * d), tail]
                bc[d, 3] = send(held, held, y_dev[d])
                held = gb.at[x, ymod(-2 * d), parts[d]]
                bc[d, 4] = send(held, held, y_far[d])
        for d in (1, -1) if s < 4 else (1,):
            b_cross(d * s, s > 2)

    def gz_step(s):
        for d in (1, -1):
            gz[d, s].wait_recv()
            if s == 2:
                held = ga.at[zmod(-2 * d), h]
                gz[d, 3] = send(held, held, z_dev[d])
                held = ga.at[zmod(-2 * d), h, zhalf[d]]
                gz[d, 4] = send(held, held, z_far[d])
        for d in (1, -1) if s < 4 else (1,):
            held = ga.at[zmod(-d * s), h]
            gs[d * s] = send(held, held, sibling)

    def a_step(s, rx):
        for d in (1, -1):
            if s == 0:
                if d == 1:
                    ax[rx].wait_recv()
            elif (d, s, rx) in ac:
                ac[d, s, rx].wait_recv()
            else:
                continue
            held = gb.at[xmod(-rx), ymod(-d * s), head]
            if s < 3:
                ac[d, s + 1, rx] = send(held, held, y_dev[d])
            if s == 2 and (rx in (0, 1)) == (d == 1):
                ac[d, 4, rx] = send(held, held, y_far[d])

    a_step(0, 1)
    a_step(0, -1)
    b_step(2)
    b_step(1)
    a_step(0, 2)
    a_step(1, 0)
    gz_step(2)
    gz_step(1)
    a_step(1, 1)
    a_step(1, -1)
    b_step(3)
    b_step(4)
    a_step(1, 2)
    a_step(2, 0)
    a_step(2, 1)
    a_step(2, -1)
    b_relay(1)
    b_relay(-1)
    b_relay(2)
    b_relay(-2)
    a_step(2, 2)
    gz_step(3)
    gz_step(4)
    for s in (3, 4):
        for rx in (0, 1, -1, 2):
            a_step(s, rx)
    for copy in gs.values():
        copy.wait_recv()
    for (s, d), copy in bx.items():
        if s == 0 or abs(d) == 2 or abs(s) > 2:
            copy.wait_recv()

    def square(qq, total):
        xx, yy = qq // NYL, qq % NYL
        for half in range(2):
            right = jnp.concatenate(
                [gb[xx, 4 * half + yy], gb[xx, 4 * half + 2 + yy]], axis=0
            )
            total = total + jnp.dot(ga[qq, half], right, preferred_element_type=F32)
        return total

    total = jnp.zeros((R, W), F32)
    for qq in range(8):
        total = square(qq, total)
    poly = (quintic_b * gb[x, y].astype(F32) + quintic_c * total).astype(BF16)
    pb[q, h] = poly

    pc, ps = {}, {}
    for k in (2, 6, 1, 4, 3, 7, 5):
        pc[k] = send(pb.at[q, h], pb.at[q, h], q_dev(k))
    ps[0] = send(pb.at[q, h], pb.at[q, h], sibling)

    drain_at = len(pending) - 8
    for copy in pending[:drain_at]:
        copy.wait_send()
    del pending[:drain_at]
    for k in range(1, 8):
        for bit in range(2):
            rs_copy(q_of(k), q, bit).wait_send()
    for zz in range(NZ):
        for bit in range(2):
            sib_copy(zz, 2 * (1 - h) + bit).wait_send()

    def turn(qq, half):
        turned = pb[qq, half].astype(F32).T.astype(BF16)
        columns = pl.ds(pl.multiple_of(qq * R, R), R)
        for part in range(2):
            pt[2 * half + part, :, columns] = turned[part * R : (part + 1) * R]

    turn(q, h)

    def from_q(k):
        dx, dy = k // 2, k % 2
        return ((x - dx + NX) % NX) * NYL + (yl + dy) % NYL

    for k in (2, 6, 1, 4, 3, 7, 5):
        held = pb.at[from_q(k), h]
        pc[k].wait_recv()
        ps[k] = send(held, held, sibling)
        turn(from_q(k), h)
    for k in (0, 2, 6, 1, 4, 3, 7, 5):
        ps[k].wait_recv()
        turn(from_q(k), 1 - h)

    zr, yr = {}, {}

    def z_part(offsets):
        value = 0.0
        for half in range(2):
            left = jnp.concatenate([pb[zmod(a), half] for a in offsets], axis=0)
            right = xj[2 * half : 2 * half + 2, :, 0:CZ].reshape(W, CZ)
            value = value + jnp.dot(left, right, preferred_element_type=F32)
        for n, a in enumerate(offsets):
            zp[a % NZ] = value[n * R : (n + 1) * R]

    def y_part(offsets):
        left = jnp.concatenate([pt[yhmod(a)] for a in offsets], axis=0)
        right = xi[:, :, CZ:C].reshape(NZ * R, CY)
        value = jnp.dot(left, right, preferred_element_type=F32)
        for n, a in enumerate(offsets):
            yp[a % NYH] = value[n * R : (n + 1) * R]

    def first(d):
        return 0 if d == 1 else 1

    def z_send(d, s, c):
        n = 0 if d == 1 else 1
        value = zp[(d * (4 - s)) % NZ, halves[c]]
        for before in {2: (1, 0), 3: (2,)}.get(s, ()):
            if (d, before, c) in zr:
                zr[d, before, c].wait_recv()
                value = value + zs_in[n, before, halves[c]].astype(F32)
        zs_out[n, s, halves[c]] = value.astype(BF16)
        to = z_dev[d] if s else z_far[d]
        zr[d, s, c] = send(zs_out.at[n, s, halves[c]], zs_in.at[n, s, halves[c]], to)

    def y_send(d, s, c):
        n = 0 if d == 1 else 1
        value = yp[(d * (2 - s)) % NYH, halves[c]]
        if (d, s - 1, c) in yr:
            yr[d, s - 1, c].wait_recv()
            value = value + ys_in[n, s - 1, halves[c]].astype(F32)
        ys_out[n, s, halves[c]] = value.astype(BF16)
        yr[d, s, c] = send(ys_out.at[n, s, halves[c]], ys_in.at[n, s, halves[c]], yh_dev[d])

    def z_got(d, s, c):
        zr[d, s, c].wait_recv()
        return zs_in[0 if d == 1 else 1, s, halves[c]].astype(F32)

    def y_got(d, s, c):
        yr[d, s, c].wait_recv()
        return ys_in[0 if d == 1 else 1, s, halves[c]].astype(F32)

    z_part([4])
    for d in (1, -1):
        z_send(d, 0, first(d))
    y_part([2])
    for d in (1, -1):
        y_send(d, 0, first(d))
    z_part([3, -3])
    for c in (0, 1):
        for d in (1, -1):
            z_send(d, 1, first(d) if c == 0 else 1 - first(d))
    y_part([1, -1])
    for d in (1, -1):
        y_send(d, 1, 1 - first(d))
    z_part([2, -2])
    z_part([1, -1])
    for d in (1, -1):
        z_send(d, 2, first(d))
    for d in (1, -1):
        z_send(d, 2, 1 - first(d))
    for d in (1, -1):
        y_send(d, 1, first(d))
    y_part([0])
    z_part([0])
    for d in (1, -1):
        z_send(d, 3, first(d))
    for d in (1, -1):
        z_send(d, 3, 1 - first(d))
    scale = math.sqrt(max(M, N))
    for c in (0, 1):
        rows = halves[c]
        value = yp[0, rows] + y_got(1, 1, c) + y_got(-1, 1, c)
        out_ref[rows, CZ:C] = scale * (quintic_a * xi[z, rows, CZ:C].astype(F32) + value)
    for c in (0, 1):
        rows = halves[c]
        value = zp[0, rows] + z_got(1, 3, c) + z_got(-1, 3, c)
        out_ref[rows, 0:CZ] = scale * (quintic_a * xi[z, rows, 0:CZ].astype(F32) + value)

    for copy in pending:
        copy.wait_send()


def per_device(momentum):
    return pl.pallas_call(
        kernel,
        out_shape=jax.ShapeDtypeStruct((R, C), F32),
        in_specs=[pl.BlockSpec(memory_space=pl.ANY)],
        out_specs=pl.BlockSpec(memory_space=pltpu.VMEM),
        scratch_shapes=[
            pltpu.VMEM((NZ, R, C), BF16),
            pltpu.VMEM((NYH, R, C), BF16),
            pltpu.VMEM((NZ, 2, R, R), F32),
            pltpu.VMEM((NZ, NYH, R, R), F32),
            pltpu.VMEM((NZ, NYH, R, R), F32),
            pltpu.VMEM((2, R, R), F32),
            pltpu.VMEM((NZ, 2, R, R), BF16),
            pltpu.VMEM((NZ, 2, R, R), BF16),
            pltpu.VMEM((NZ, 2, R, W), BF16),
            pltpu.VMEM((NX, NY, R, W), BF16),
            pltpu.VMEM((NZ, 2, R, W), BF16),
            pltpu.VMEM((NYH, R, NZ * R), BF16),
            pltpu.VMEM((2, 4, R, CZ), BF16),
            pltpu.VMEM((2, 4, R, CZ), BF16),
            pltpu.VMEM((2, 2, R, CY), BF16),
            pltpu.VMEM((2, 2, R, CY), BF16),
            pltpu.VMEM((NZ, R, CZ), F32),
            pltpu.VMEM((NYH, R, CY), F32),
            pltpu.SemaphoreType.DMA((SEMS,)),
            pltpu.SemaphoreType.DMA((SEMS,)),
            pltpu.SemaphoreType.DMA((NZ, 2)),
            pltpu.SemaphoreType.DMA((NZ, 2)),
            pltpu.SemaphoreType.DMA((NZ, NYH)),
            pltpu.SemaphoreType.DMA((NZ, NYH)),
            pltpu.SemaphoreType.DMA((2,)),
        ],
        compiler_params=pltpu.CompilerParams(
            collective_id=0, has_side_effects=True, vmem_limit_bytes=48 * 1024 * 1024
        ),
        cost_estimate=pl.CostEstimate(flops=2200000000, bytes_accessed=1000000, transcendentals=0),
        name="newton_schulz",
    )(momentum)


def solution(mesh):
    return jax.shard_map(
        per_device, mesh=mesh, in_specs=(P("row", "col"),), out_specs=P("row", "col"), check_vma=False
    )
```
